512 devices in a mesh: cluster: 128 (over z, y, core), rep: 4 (over x).
Axes of the slice: x: 4, y: 8, z: 8, core: 2. Of those that a mesh axis runs over, the one named last changes fastest.
Arguments:
- embeddings: float32 [131072, 1024], P(('cluster', 'rep'))
- cluster_sizes: int32 [128], P('cluster'), may hold values from 256 to 1024, as said below
- offsets: int32 [2, 128], P(None, 'cluster'), may hold values from 1 to 3, as said below
Outputs:
- best_rows: float32 [131072], P(('cluster', 'rep'))
The draws below stay inside these ranges and needn't reach their ends.
Inputs may be any that keep to these rules, and one draw needn't show every extreme that they name: `cluster_sizes`: every cluster has at least 256 rows in use; some cluster is full and some has exactly 256. A cluster's offsets in the 2 rounds are distinct; some cluster has offset 3 in the first round.
All inputs are finite; a program needn't handle non-finite values.
Results may differ from the reference program's by a relative error of at most 0.0003.
Values may be sent and summed in bfloat16 or wider, within the bound.
No kernel may reach another device: no remote copies, remote signals or barrier semaphores. Data moves between devices by JAX's collectives and lax.ppermute only.
A program may use at most 64 MiB of HBM per device.

```python
import jax
import jax.numpy as jnp
from jax import lax

D = 1024
ROUNDS = 2
SPAN = 3
ROWS = 1024
CLUSTERS = 128


def draw_embeddings(key, part):
    key = jax.random.fold_in(key, 11)
    keys = jax.random.split(key, 8)
    key_base, key_noise, key_scale, key_copy = (keys[0], keys[1], keys[2], keys[3])
    key_reach, key_slot, key_fresh, key_gain = (keys[4], keys[5], keys[6], keys[7])
    total = CLUSTERS * ROWS
    base = jax.random.normal(key_base, (CLUSTERS, D), jnp.float32)
    centre = base + 0.9 * jnp.roll(base, -1, axis=0) + 0.6 * jnp.roll(base, -2, axis=0)
    noise = jax.random.normal(key_noise, (total, D), jnp.float32)
    scales = jnp.exp(jax.random.uniform(key_scale, (total, 1), jnp.float32, -0.9, 0.5))
    drawn = 0.5 * jnp.repeat(centre, ROWS, axis=0) + noise * scales
    row_ids = jnp.arange(total, dtype=jnp.int32)
    home = row_ids // ROWS
    slot = row_ids % ROWS
    reach = jax.random.randint(key_reach, (total,), 1, SPAN + 1, jnp.int32)
    shuffled = jax.random.permutation(key_slot, ROWS).astype(jnp.int32)
    source = ((home + reach) % CLUSTERS * ROWS + shuffled[slot]).astype(jnp.int32)
    copied = jax.random.randint(key_copy, (total,), 0, 4, jnp.int32) == 0
    fresh = jax.random.normal(key_fresh, (total, D), jnp.float32)
    near = drawn[source] + 0.25 * fresh
    mixed = jnp.where(copied[:, None], near, drawn)
    gains = jnp.exp(jax.random.uniform(key_gain, (total, 1), jnp.float32, -2.0, 2.0))
    return mixed * gains


def draw_cluster_sizes(key, part):
    key = jax.random.fold_in(key, 12)
    key_sizes, key_pick = jax.random.split(key, 2)
    sizes = jax.random.randint(key_sizes, (CLUSTERS,), ROWS // 4, ROWS + 1, jnp.int32)
    picked = jax.random.randint(key_pick, (), 0, CLUSTERS, jnp.int32)
    cluster_ids = jnp.arange(CLUSTERS, dtype=jnp.int32)
    smallest = (picked + CLUSTERS // 2) % CLUSTERS
    sizes = jnp.where(cluster_ids == smallest, ROWS // 4, sizes)
    return jnp.where(cluster_ids == picked, ROWS, sizes).astype(jnp.int32)


def draw_offsets(key, part):
    key = jax.random.fold_in(key, 13)
    key_perm, key_pick = jax.random.split(key, 2)
    cluster_keys = jax.random.split(key_perm, CLUSTERS)
    orders = jax.vmap(lambda one_key: jax.random.permutation(one_key, SPAN))(cluster_keys).astype(jnp.int32) + 1
    chosen = orders[:, :ROUNDS]
    picked = jax.random.randint(key_pick, (), 0, CLUSTERS, jnp.int32)
    forced = (SPAN - jnp.arange(ROUNDS, dtype=jnp.int32))[None, :]
    cluster_ids = jnp.arange(CLUSTERS, dtype=jnp.int32)[:, None]
    chosen = jnp.where(cluster_ids == picked, forced, chosen)
    return chosen.T.astype(jnp.int32)


def setup_inputs(seed: int = 0) -> dict:
    arg_keys = jax.random.split(jax.random.key(seed), 4)
    return {
        "embeddings": draw_embeddings(jax.random.fold_in(arg_keys[3], 71), 0),
        "cluster_sizes": draw_cluster_sizes(jax.random.fold_in(arg_keys[3], 71), 0),
        "offsets": draw_offsets(jax.random.fold_in(arg_keys[3], 71), 0),
    }


def reference(embeddings, cluster_sizes, offsets):
    row_norms = jnp.sqrt(lax.optimization_barrier(jnp.sum(embeddings * embeddings, axis=1, keepdims=True)) + 1e-06)
    unit_rows = (embeddings / row_norms).astype(jnp.bfloat16).reshape(CLUSTERS, ROWS, D)
    positions = jnp.arange(ROWS, dtype=jnp.int32)
    valid = positions[None, :] < cluster_sizes[:, None]
    cluster_ids = jnp.arange(CLUSTERS, dtype=jnp.int32)
    row_best = jnp.full((CLUSTERS, ROWS), -4.0, jnp.float32)
    for round_index in range(ROUNDS):
        partner_ids = ((cluster_ids + offsets[round_index]) % CLUSTERS).astype(jnp.int32)

        def pair_maxima(cluster_index):
            partner_index = partner_ids[cluster_index]
            own_rows = unit_rows[cluster_index].astype(jnp.float32)
            partner_rows = unit_rows[partner_index].astype(jnp.float32)
            scores = jnp.dot(own_rows, partner_rows.T, precision=lax.Precision.HIGHEST, preferred_element_type=jnp.float32)
            allowed = valid[cluster_index][:, None] & valid[partner_index][None, :]
            scores = jnp.where(allowed, scores, jnp.float32(-4.0))
            return (lax.optimization_barrier(jnp.max(scores, axis=1)), lax.optimization_barrier(jnp.max(scores, axis=0)))
        row_max, column_max = lax.map(pair_maxima, cluster_ids)
        column_back = jnp.full((CLUSTERS, ROWS), -4.0, jnp.float32).at[partner_ids].max(column_max)
        row_best = jnp.maximum(row_best, jnp.maximum(row_max, column_back))
    return jnp.where(valid, row_best, jnp.float32(0.0)).reshape(CLUSTERS * ROWS)
```

```python
import jax
import jax.numpy as jnp
from jax import lax
from jax.experimental import pallas as pl
from jax.experimental.pallas import tpu as pltpu
from jax.sharding import PartitionSpec as P

SPAN = 3
META = 16
VMEM = pl.BlockSpec(memory_space=pltpu.VMEM)
SMEM = pl.BlockSpec(memory_space=pltpu.SMEM)


def norm_kernel(size_ref, offset_ref, rows_ref, unit_ref, payload_ref):
    rows, width = rows_ref.shape
    values = rows_ref[...]
    norms = jnp.sqrt(jnp.sum(values * values, axis=1, keepdims=True) + 1e-06)
    unit = (values / norms).astype(jnp.bfloat16)
    unit_ref[...] = unit
    payload_ref[0:rows, :] = unit
    used = jnp.clip(size_ref[0] - lax.axis_index("rep") * rows, 0, rows)
    line = lax.broadcasted_iota(jnp.int32, (META, width), 0)
    meta = jnp.where(line == 0, used, 0)
    for k in range(offset_ref.shape[0]):
        meta = jnp.where(line == k + 1, offset_ref[k, 0], meta)
    payload_ref[rows:, :] = meta.astype(jnp.float32).astype(jnp.bfloat16)


def neighbour_bias(offset_ref, payload_ref, delta, rows):
    meta = payload_ref[rows:, 0:128].astype(jnp.float32)
    own = jnp.bool_(False)
    theirs = jnp.zeros((1, 128), jnp.bool_)
    for k in range(offset_ref.shape[0]):
        own = own | (offset_ref[k, 0] == delta)
        theirs = theirs | (meta[k + 1 : k + 2, :] == (-delta).astype(jnp.float32))
    own_flag = jnp.where(own, 1.0, 0.0)
    flag = jnp.where(delta > 0, own_flag, jnp.where(theirs, 1.0, 0.0))
    used = meta[0:1, :] * flag
    line = lax.broadcasted_iota(jnp.int32, (rows, 128), 0).astype(jnp.float32)
    return jnp.where(line < used, 0.0, -8.0)


def maxima_kernel(offset_ref, *refs):
    pieces, payloads, best_ref = refs[:4], refs[4:-1], refs[-1]
    rows = pieces[0].shape[0]
    odd = lax.rem(lax.axis_index("cluster"), 2)
    rep = lax.axis_index("rep")
    deltas = (1 - 2 * odd, jnp.int32(2), jnp.int32(-2), 3 - 2 * odd, -1 - 2 * odd, 6 * odd - 3)
    biases = [neighbour_bias(offset_ref, p, d, rows) for p, d in zip(payloads, deltas)]
    for away, piece in enumerate(pieces):
        best = jnp.full((1, rows), -4.0, jnp.float32)
        for payload, bias in zip(payloads, biases):
            scores = lax.dot_general(
                payload[0:rows, :], piece[...], (((1,), (1,)), ((), ())), preferred_element_type=jnp.float32
            )
            wide = jnp.concatenate([bias] * (rows // 128), axis=1)
            best = jnp.maximum(best, jnp.max(scores + wide, axis=0, keepdims=True))
        best_ref[pl.ds(lax.rem(rep + away, 4), 1), :] = best


def over_cluster(block, source):
    n = lax.axis_size("cluster")
    return lax.ppermute(block, "cluster", [(source(i) % n, i) for i in range(n)])


def over_rep(block, away):
    n = lax.axis_size("rep")
    return lax.ppermute(block, "rep", [((i + away) % n, i) for i in range(n)])


def shards(embeddings, cluster_sizes, offsets):
    rows, width = embeddings.shape
    unit, payload = pl.pallas_call(
        norm_kernel,
        out_shape=(
            jax.ShapeDtypeStruct((rows, width), jnp.bfloat16),
            jax.ShapeDtypeStruct((rows + META, width), jnp.bfloat16),
        ),
        in_specs=[SMEM, SMEM, VMEM],
        out_specs=(VMEM, VMEM),
        name="unit_rows",
    )(cluster_sizes, offsets, embeddings)
    pieces = [unit] + [over_rep(unit, away) for away in (1, 2, 3)]
    ahead = over_cluster(payload, lambda i: i + 2)
    behind = over_cluster(payload, lambda i: i - 2)
    far = over_cluster(payload, lambda i: i + 3 if i % 2 else i - 3)
    mate = over_cluster(payload, lambda i: i ^ 1)
    ahead_mate = over_cluster(ahead, lambda i: i ^ 1)
    behind_mate = over_cluster(behind, lambda i: i ^ 1)
    best = pl.pallas_call(
        maxima_kernel,
        out_shape=jax.ShapeDtypeStruct((4, rows), jnp.float32),
        in_specs=[SMEM] + [VMEM] * 10,
        out_specs=VMEM,
        name="maxima",
        compiler_params=pltpu.CompilerParams(vmem_limit_bytes=32 * 1024 * 1024),
    )(offsets, *pieces, mate, ahead, behind, ahead_mate, behind_mate, far)
    row_best = jnp.max(lax.all_to_all(best, "rep", 0, 0), axis=0)
    row_ids = lax.axis_index("rep") * rows + jnp.arange(rows, dtype=jnp.int32)
    return jnp.where(row_ids < cluster_sizes[0], row_best, 0.0)


def solution(mesh):
    return jax.shard_map(
        shards,
        mesh=mesh,
        in_specs=(P(("cluster", "rep"), None), P("cluster"), P(None, "cluster")),
        out_specs=P(("cluster", "rep")),
        check_vma=False,
    )
```

```python
import jax
import jax.numpy as jnp
from jax import lax
from jax.experimental import pallas as pl
from jax.experimental.pallas import tpu as pltpu
from jax.sharding import PartitionSpec as P

META = 16
VMEM = pl.BlockSpec(memory_space=pltpu.VMEM)
SMEM = pl.BlockSpec(memory_space=pltpu.SMEM)
TAKEN = ((2, 2, 2, 2), (-1, -3, -1, -3), (1, 3, -3, -1))


def norm_kernel(size_ref, offset_ref, rows_ref, copies_ref, payload_ref):
    rows, width = rows_ref.shape
    values = rows_ref[...]
    norms = jnp.sqrt(jnp.sum(values * values, axis=1, keepdims=True) + 1e-06)
    unit = (values / norms).astype(jnp.bfloat16)
    for k in range(copies_ref.shape[0]):
        copies_ref[k] = unit
    payload_ref[0:rows, :] = unit
    used = jnp.clip(size_ref[0] - lax.axis_index("rep") * rows, 0, rows)
    line = lax.broadcasted_iota(jnp.int32, (META, width), 0)
    meta = jnp.where(line == 0, used, 0)
    for k in range(offset_ref.shape[1]):
        meta = jnp.where(line == k + 1, offset_ref[0, k], meta)
    payload_ref[rows:, :] = meta.astype(jnp.float32).astype(jnp.bfloat16)


def maxima_kernel(size_ref, offset_ref, own_ref, *refs):
    payloads, row_ref, column_refs = refs[:3], refs[3], refs[4:]
    reps, rows, _ = own_ref.shape
    place = lax.rem(lax.axis_index("cluster"), 4)
    best = [jnp.full((1, rows), -4.0, jnp.float32) for _ in range(reps)]
    lane = lax.broadcasted_iota(jnp.int32, (1, rows), 1)
    line = lax.broadcasted_iota(jnp.int32, (rows, 128), 0).astype(jnp.float32)
    for payload, column_ref, taken in zip(payloads, column_refs, TAKEN):
        delta = jnp.int32(taken[0])
        for k in range(1, 4):
            delta = jnp.where(place == k, taken[k], delta)
        meta = payload[rows:, 0:128].astype(jnp.float32)
        mine = jnp.float32(0.0)
        theirs = jnp.zeros((1, 128), jnp.float32)
        for k in range(offset_ref.shape[1]):
            mine = jnp.where(offset_ref[0, k] == delta, 1.0, mine)
            theirs = jnp.where(meta[k + 1 : k + 2, :] == (-delta).astype(jnp.float32), 1.0, theirs)
        paired = jnp.where(delta > 0, mine, theirs)
        row_bias = jnp.where(line < meta[0:1, :] * paired, 0.0, -8.0)
        row_bias = jnp.concatenate([row_bias] * (rows // 128), axis=1)
        found = jnp.full((rows, 128), -4.0, jnp.float32)
        for k in range(reps):
            scores = lax.dot_general(
                payload[0:rows, :], own_ref[k], (((1,), (1,)), ((), ())), preferred_element_type=jnp.float32
            )
            best[k] = jnp.maximum(best[k], jnp.max(scores + row_bias, axis=0, keepdims=True))
            lane_bias = jnp.where(lane + k * rows < size_ref[0], 0.0, -8.0)
            scores = scores + lane_bias
            for piece in range(rows // 128):
                found = jnp.maximum(found, scores[:, piece * 128 : (piece + 1) * 128])
        column = jnp.max(found.T, axis=0, keepdims=True)
        flags = jnp.concatenate([paired] * (rows // 128), axis=1)
        column_ref[...] = jnp.where(flags > 0.5, column, -4.0)
    for k in range(reps):
        row_ref[k] = best[k]


def shifted(block, moves):
    n = lax.axis_size("cluster")
    return lax.ppermute(block, "cluster", [((i + moves[i % 4]) % n, i) for i in range(n)])


def returned(block, moves):
    n = lax.axis_size("cluster")
    return lax.ppermute(block, "cluster", [(i, (i + moves[i % 4]) % n) for i in range(n)])


def shards(embeddings, cluster_sizes, offsets):
    rows, width = embeddings.shape
    reps = lax.axis_size("rep")
    flat_offsets = offsets.T
    copies, payload = pl.pallas_call(
        norm_kernel,
        out_shape=(
            jax.ShapeDtypeStruct((reps, rows, width), jnp.bfloat16),
            jax.ShapeDtypeStruct((rows + META, width), jnp.bfloat16),
        ),
        in_specs=[SMEM, SMEM, VMEM],
        out_specs=(VMEM, VMEM),
        name="unit_rows",
        compiler_params=pltpu.CompilerParams(vmem_limit_bytes=32 * 1024 * 1024),
    )(cluster_sizes, flat_offsets, embeddings)
    own = lax.all_to_all(copies, "rep", 0, 0, tiled=True)
    taken = [shifted(payload, moves) for moves in TAKEN]
    row_part, *column_parts = pl.pallas_call(
        maxima_kernel,
        out_shape=(jax.ShapeDtypeStruct((reps, 1, rows), jnp.float32),)
        + (jax.ShapeDtypeStruct((1, rows), jnp.float32),) * 3,
        in_specs=[SMEM, SMEM] + [VMEM] * 4,
        out_specs=(VMEM,) * 4,
        name="maxima",
        compiler_params=pltpu.CompilerParams(vmem_limit_bytes=32 * 1024 * 1024),
    )(cluster_sizes, flat_offsets, own, *taken)
    row_best = jnp.max(lax.all_to_all(row_part, "rep", 0, 0, tiled=True), axis=0)
    for part, moves in zip(column_parts, TAKEN):
        row_best = jnp.maximum(row_best, returned(part, moves))
    row_ids = lax.axis_index("rep") * rows + jnp.arange(rows, dtype=jnp.int32)
    return jnp.where(row_ids < cluster_sizes[0], row_best[0], 0.0)


def solution(mesh):
    return jax.shard_map(
        shards,
        mesh=mesh,
        in_specs=(P(("cluster", "rep"), None), P("cluster"), P(None, "cluster")),
        out_specs=P(("cluster", "rep")),
        check_vma=False,
    )
```

```python
import jax
import jax.numpy as jnp
from jax import lax
from jax.experimental import pallas as pl
from jax.experimental.pallas import tpu as pltpu
from jax.sharding import PartitionSpec as P

META = 16
CHUNKS = 4
VMEM = pl.BlockSpec(memory_space=pltpu.VMEM)
SMEM = pl.BlockSpec(memory_space=pltpu.SMEM)
HBM = pl.BlockSpec(memory_space=pltpu.HBM)
WIDE = pltpu.CompilerParams(vmem_limit_bytes=60 * 1024 * 1024)
SMALL = pltpu.CompilerParams(vmem_limit_bytes=12 * 1024 * 1024)


def norm_kernel(size_ref, offset_ref, rows_ref, copies_ref, payload_ref, size, offset, raw, unit, in_sems, out_sems):
    reps, rows, width = copies_ref.shape
    step = rows // CHUNKS
    loads = [
        pltpu.make_async_copy(rows_ref.at[pl.ds(c * step, step)], raw.at[pl.ds(c * step, step)], in_sems.at[c])
        for c in range(CHUNKS)
    ]
    loads.append(pltpu.make_async_copy(size_ref, size, in_sems.at[CHUNKS]))
    loads.append(pltpu.make_async_copy(offset_ref, offset, in_sems.at[CHUNKS + 1]))
    for load in loads:
        load.start()
    stores = []

    def store(source, target):
        copy = pltpu.make_async_copy(source, target, out_sems.at[len(stores)])
        copy.start()
        stores.append(copy)

    for c in range(CHUNKS):
        part = pl.ds(c * step, step)
        loads[c].wait()
        values = raw[part, :]
        norms = jnp.sqrt(jnp.sum(values * values, axis=1, keepdims=True) + 1e-06)
        unit[part, :] = (values * (1.0 / norms)).astype(jnp.bfloat16)
        for k in range(reps):
            store(unit.at[part], copies_ref.at[k, part])
        store(unit.at[part], payload_ref.at[part])
    loads[CHUNKS].wait()
    loads[CHUNKS + 1].wait()
    used = jnp.clip(size[0, 0] - lax.axis_index("rep") * rows, 0, rows)
    line = lax.broadcasted_iota(jnp.int32, (META, width), 0)
    meta = jnp.where(line == 0, used, 0)
    for k in range(offset_ref.shape[1]):
        meta = jnp.where(line == k + 1, offset[0, k], meta)
    unit[rows:, :] = meta.astype(jnp.float32).astype(jnp.bfloat16)
    store(unit.at[pl.ds(rows, META)], payload_ref.at[pl.ds(rows, META)])
    for copy in stores:
        copy.wait()


def row_bias(offset_ref, payload, delta, rows):
    meta = payload[rows : rows + META, 0:128].astype(jnp.float32)
    mine = jnp.float32(0.0)
    theirs = jnp.zeros((1, 128), jnp.float32)
    for k in range(offset_ref.shape[1]):
        mine = jnp.where(offset_ref[0, k] == delta, 1.0, mine)
        theirs = jnp.where(meta[k + 1 : k + 2, :] == (-delta).astype(jnp.float32), 1.0, theirs)
    paired = jnp.where(delta > 0, mine, theirs)
    line = lax.broadcasted_iota(jnp.int32, (rows, 128), 0).astype(jnp.float32)
    bias = jnp.where(line < meta[0:1, :] * paired, 0.0, -8.0)
    return jnp.concatenate([bias] * (rows // 128), axis=1)


def score(offset_ref, own_ref, payload, delta, best):
    reps, rows, _ = own_ref.shape
    bias = row_bias(offset_ref, payload, delta, rows)
    for k in range(reps):
        scores = lax.dot_general(
            payload[0:rows, :], own_ref[k], (((1,), (1,)), ((), ())), preferred_element_type=jnp.float32
        )
        best[k] = jnp.maximum(best[k], jnp.max(scores + bias, axis=0, keepdims=True))


def early_kernel(offset_ref, own_ref, ahead_ref, behind_ref, best_ref):
    reps, rows, _ = own_ref.shape
    best = [jnp.full((1, rows), -4.0, jnp.float32) for _ in range(reps)]
    score(offset_ref, own_ref, ahead_ref, jnp.int32(2), best)
    score(offset_ref, own_ref, behind_ref, jnp.int32(-2), best)
    for k in range(reps):
        best_ref[k] = best[k]


def late_kernel(
    offset_ref, own_ref, far_ref, mate_ref, ahead_ref, behind_ref, early_ref, best_ref, ahead, behind, sems
):
    reps, rows, _ = own_ref.shape
    odd = lax.rem(lax.axis_index("cluster"), 2)
    loads = [
        pltpu.make_async_copy(ahead_ref, ahead, sems.at[0]),
        pltpu.make_async_copy(behind_ref, behind, sems.at[1]),
    ]
    for load in loads:
        load.start()
    best = [early_ref[k] for k in range(reps)]
    score(offset_ref, own_ref, far_ref, 6 * odd - 3, best)
    score(offset_ref, own_ref, mate_ref, 1 - 2 * odd, best)
    loads[0].wait()
    score(offset_ref, own_ref, ahead, 3 - 2 * odd, best)
    loads[1].wait()
    score(offset_ref, own_ref, behind, -1 - 2 * odd, best)
    for k in range(reps):
        best_ref[k] = best[k]


def over_cluster(block, even, odd):
    n = lax.axis_size("cluster")
    return lax.ppermute(block, "cluster", [((i + (odd if i % 2 else even)) % n, i) for i in range(n)])


def shards(embeddings, cluster_sizes, offsets):
    rows, width = embeddings.shape
    reps = lax.axis_size("rep")
    flat_offsets = offsets.T
    flat_sizes = cluster_sizes.reshape(1, 1)
    payload_shape = jax.ShapeDtypeStruct((rows + META, width), jnp.bfloat16)
    copies, payload = pl.pallas_call(
        norm_kernel,
        out_shape=(jax.ShapeDtypeStruct((reps, rows, width), jnp.bfloat16), payload_shape),
        in_specs=[HBM, HBM, HBM],
        out_specs=(HBM, HBM),
        scratch_shapes=[
            pltpu.SMEM(flat_sizes.shape, jnp.int32),
            pltpu.SMEM(flat_offsets.shape, jnp.int32),
            pltpu.VMEM((rows, width), jnp.float32),
            pltpu.VMEM((rows + META, width), jnp.bfloat16),
            pltpu.SemaphoreType.DMA((CHUNKS + 2,)),
            pltpu.SemaphoreType.DMA((CHUNKS * (reps + 1) + 1,)),
        ],
        name="unit_rows",
        compiler_params=WIDE,
    )(flat_sizes, flat_offsets, embeddings)
    own = lax.all_to_all(copies, "rep", 0, 0, tiled=True)
    behind = over_cluster(payload, -2, -2)
    ahead = over_cluster(payload, 2, 2)
    mate = over_cluster(payload, 1, -1)
    far = over_cluster(payload, -3, 3)
    ahead_mate = over_cluster(ahead, 1, -1)
    behind_mate = over_cluster(behind, 1, -1)
    part_shape = jax.ShapeDtypeStruct((reps, 1, rows), jnp.float32)
    part = pl.pallas_call(
        early_kernel,
        out_shape=part_shape,
        in_specs=[SMEM] + [VMEM] * 3,
        out_specs=VMEM,
        name="early_maxima",
        compiler_params=SMALL,
    )(flat_offsets, own, ahead, behind)
    part = pl.pallas_call(
        late_kernel,
        out_shape=part_shape,
        in_specs=[SMEM] + [VMEM] * 3 + [HBM] * 2 + [VMEM],
        out_specs=VMEM,
        scratch_shapes=[
            pltpu.VMEM((rows + META, width), jnp.bfloat16),
            pltpu.VMEM((rows + META, width), jnp.bfloat16),
            pltpu.SemaphoreType.DMA((2,)),
        ],
        name="late_maxima",
        compiler_params=SMALL,
    )(flat_offsets, own, far, mate, ahead_mate, behind_mate, part)
    row_best = jnp.max(lax.all_to_all(part, "rep", 0, 0, tiled=True), axis=(0, 1))
    row_ids = lax.axis_index("rep") * rows + jnp.arange(rows, dtype=jnp.int32)
    return jnp.where(row_ids < cluster_sizes[0], row_best, 0.0)


def solution(mesh):
    return jax.shard_map(
        shards,
        mesh=mesh,
        in_specs=(P(("cluster", "rep"), None), P("cluster"), P(None, "cluster")),
        out_specs=P(("cluster", "rep")),
        check_vma=False,
    )
```

```python
import jax
import jax.numpy as jnp
from jax import lax
from jax.experimental import pallas as pl
from jax.experimental.pallas import tpu as pltpu
from jax.sharding import PartitionSpec as P

META = 16
CHUNKS = 4
VMEM = pl.BlockSpec(memory_space=pltpu.VMEM)
SMEM = pl.BlockSpec(memory_space=pltpu.SMEM)
HBM = pl.BlockSpec(memory_space=pltpu.HBM)
WIDE = pltpu.CompilerParams(vmem_limit_bytes=60 * 1024 * 1024)
SMALL = pltpu.CompilerParams(vmem_limit_bytes=12 * 1024 * 1024)


def norm_kernel(size_ref, offset_ref, rows_ref, copies_ref, payload_ref, size, offset, raw, unit, in_sems, out_sems):
    reps, rows, width = copies_ref.shape
    step = rows // CHUNKS
    loads = [
        pltpu.make_async_copy(rows_ref.at[pl.ds(c * step, step)], raw.at[pl.ds(c * step, step)], in_sems.at[c])
        for c in range(CHUNKS)
    ]
    loads.append(pltpu.make_async_copy(size_ref, size, in_sems.at[CHUNKS]))
    loads.append(pltpu.make_async_copy(offset_ref, offset, in_sems.at[CHUNKS + 1]))
    for load in loads:
        load.start()
    stores = []

    def store(source, target):
        copy = pltpu.make_async_copy(source, target, out_sems.at[len(stores)])
        copy.start()
        stores.append(copy)

    for c in range(CHUNKS):
        part = pl.ds(c * step, step)
        loads[c].wait()
        values = raw[part, :]
        norms = jnp.sqrt(jnp.sum(values * values, axis=1, keepdims=True) + 1e-06)
        unit[part, :] = (values * (1.0 / norms)).astype(jnp.bfloat16)
        for k in range(reps):
            store(unit.at[part], copies_ref.at[k, part])
        store(unit.at[part], payload_ref.at[part])
    loads[CHUNKS].wait()
    loads[CHUNKS + 1].wait()
    used = jnp.clip(size[0, 0] - lax.axis_index("rep") * rows, 0, rows)
    line = lax.broadcasted_iota(jnp.int32, (META, width), 0)
    meta = jnp.where(line == 0, used, 0)
    for k in range(offset_ref.shape[1]):
        meta = jnp.where(line == k + 1, offset[0, k], meta)
    unit[rows:, :] = meta.astype(jnp.float32).astype(jnp.bfloat16)
    store(unit.at[pl.ds(rows, META)], payload_ref.at[pl.ds(rows, META)])
    for copy in stores:
        copy.wait()


def row_bias(offset_ref, payload, delta, rows):
    meta = payload[rows : rows + META, 0:128].astype(jnp.float32)
    mine = jnp.float32(0.0)
    theirs = jnp.zeros((1, 128), jnp.float32)
    for k in range(offset_ref.shape[1]):
        mine = jnp.where(offset_ref[0, k] == delta, 1.0, mine)
        theirs = jnp.where(meta[k + 1 : k + 2, :] == (-delta).astype(jnp.float32), 1.0, theirs)
    paired = jnp.where(delta > 0, mine, theirs)
    line = lax.broadcasted_iota(jnp.int32, (rows, 128), 0).astype(jnp.float32)
    bias = jnp.where(line < meta[0:1, :] * paired, 0.0, -8.0)
    return jnp.concatenate([bias] * (rows // 128), axis=1)


def score(offset_ref, own_ref, payload, delta, best):
    reps, rows, _ = own_ref.shape
    bias = row_bias(offset_ref, payload, delta, rows)
    for k in range(reps):
        scores = lax.dot_general(
            payload[0:rows, :], own_ref[k], (((1,), (1,)), ((), ())), preferred_element_type=jnp.float32
        )
        best[k] = jnp.maximum(best[k], jnp.max(scores + bias, axis=0, keepdims=True))


def early_kernel(offset_ref, own_ref, mate_ref, ahead_ref, behind_ref, best_ref):
    reps, rows, _ = own_ref.shape
    odd = lax.rem(lax.axis_index("cluster"), 2)
    best = [jnp.full((1, rows), -4.0, jnp.float32) for _ in range(reps)]
    score(offset_ref, own_ref, mate_ref, 1 - 2 * odd, best)
    score(offset_ref, own_ref, ahead_ref, jnp.int32(2), best)
    score(offset_ref, own_ref, behind_ref, jnp.int32(-2), best)
    for k in range(reps):
        best_ref[k] = best[k]


def late_kernel(offset_ref, own_ref, far_ref, ahead_ref, behind_ref, early_ref, best_ref, behind, ahead, far, sems):
    reps, rows, _ = own_ref.shape
    odd = lax.rem(lax.axis_index("cluster"), 2)
    loads = [
        pltpu.make_async_copy(behind_ref, behind, sems.at[0]),
        pltpu.make_async_copy(ahead_ref, ahead, sems.at[1]),
        pltpu.make_async_copy(far_ref, far, sems.at[2]),
    ]
    loads[0].start()
    loads[1].start()
    best = [early_ref[k] for k in range(reps)]
    loads[0].wait()
    loads[2].start()
    score(offset_ref, own_ref, behind, -1 - 2 * odd, best)
    loads[1].wait()
    score(offset_ref, own_ref, ahead, 3 - 2 * odd, best)
    loads[2].wait()
    score(offset_ref, own_ref, far, 6 * odd - 3, best)
    for k in range(reps):
        best_ref[k] = best[k]


def over_cluster(block, even, odd):
    n = lax.axis_size("cluster")
    return lax.ppermute(block, "cluster", [((i + (odd if i % 2 else even)) % n, i) for i in range(n)])


def shards(embeddings, cluster_sizes, offsets):
    rows, width = embeddings.shape
    reps = lax.axis_size("rep")
    flat_offsets = offsets.T
    flat_sizes = cluster_sizes.reshape(1, 1)
    payload_shape = jax.ShapeDtypeStruct((rows + META, width), jnp.bfloat16)
    copies, payload = pl.pallas_call(
        norm_kernel,
        out_shape=(jax.ShapeDtypeStruct((reps, rows, width), jnp.bfloat16), payload_shape),
        in_specs=[HBM, HBM, HBM],
        out_specs=(HBM, HBM),
        scratch_shapes=[
            pltpu.SMEM(flat_sizes.shape, jnp.int32),
            pltpu.SMEM(flat_offsets.shape, jnp.int32),
            pltpu.VMEM((rows, width), jnp.float32),
            pltpu.VMEM((rows + META, width), jnp.bfloat16),
            pltpu.SemaphoreType.DMA((CHUNKS + 2,)),
            pltpu.SemaphoreType.DMA((CHUNKS * (reps + 1) + 1,)),
        ],
        name="unit_rows",
        compiler_params=WIDE,
    )(flat_sizes, flat_offsets, embeddings)
    own = lax.all_to_all(copies, "rep", 0, 0, tiled=True)
    behind = over_cluster(payload, -2, -2)
    ahead = over_cluster(payload, 2, 2)
    mate = over_cluster(payload, 1, -1)
    far = over_cluster(payload, -3, 3)
    ahead_mate = over_cluster(ahead, 1, -1)
    behind_mate = over_cluster(behind, 1, -1)
    part_shape = jax.ShapeDtypeStruct((reps, 1, rows), jnp.float32)
    part = pl.pallas_call(
        early_kernel,
        out_shape=part_shape,
        in_specs=[SMEM] + [VMEM] * 4,
        out_specs=VMEM,
        name="early_maxima",
        compiler_params=SMALL,
    )(flat_offsets, own, mate, ahead, behind)
    part = pl.pallas_call(
        late_kernel,
        out_shape=part_shape,
        in_specs=[SMEM, VMEM] + [HBM] * 3 + [VMEM],
        out_specs=VMEM,
        scratch_shapes=[
            pltpu.VMEM((rows + META, width), jnp.bfloat16),
            pltpu.VMEM((rows + META, width), jnp.bfloat16),
            pltpu.VMEM((rows + META, width), jnp.bfloat16),
            pltpu.SemaphoreType.DMA((3,)),
        ],
        name="late_maxima",
        compiler_params=SMALL,
    )(flat_offsets, own, far, ahead_mate, behind_mate, part)
    row_best = jnp.max(lax.all_to_all(part, "rep", 0, 0, tiled=True), axis=(0, 1))
    row_ids = lax.axis_index("rep") * rows + jnp.arange(rows, dtype=jnp.int32)
    return jnp.where(row_ids < cluster_sizes[0], row_best, 0.0)


def solution(mesh):
    return jax.shard_map(
        shards,
        mesh=mesh,
        in_specs=(P(("cluster", "rep"), None), P("cluster"), P(None, "cluster")),
        out_specs=P(("cluster", "rep")),
        check_vma=False,
    )
```

```python
import jax
import jax.numpy as jnp
from jax import lax
from jax.experimental import pallas as pl
from jax.experimental.pallas import tpu as pltpu
from jax.sharding import PartitionSpec as P

META = 16
CHUNKS = 4
VMEM = pl.BlockSpec(memory_space=pltpu.VMEM)
SMEM = pl.BlockSpec(memory_space=pltpu.SMEM)
HBM = pl.BlockSpec(memory_space=pltpu.HBM)
WIDE = pltpu.CompilerParams(vmem_limit_bytes=60 * 1024 * 1024)
SMALL = pltpu.CompilerParams(vmem_limit_bytes=12 * 1024 * 1024)


def norm_kernel(size_ref, offset_ref, rows_ref, copies_ref, payload_ref, size, offset, raw, unit, in_sems, out_sems):
    reps, rows, width = copies_ref.shape
    step = rows // CHUNKS
    loads = [
        pltpu.make_async_copy(rows_ref.at[pl.ds(c * step, step)], raw.at[pl.ds(c * step, step)], in_sems.at[c])
        for c in range(CHUNKS)
    ]
    loads.append(pltpu.make_async_copy(size_ref, size, in_sems.at[CHUNKS]))
    loads.append(pltpu.make_async_copy(offset_ref, offset, in_sems.at[CHUNKS + 1]))
    for load in loads:
        load.start()
    stores = []

    def store(source, target):
        copy = pltpu.make_async_copy(source, target, out_sems.at[len(stores)])
        copy.start()
        stores.append(copy)

    for c in range(CHUNKS):
        part = pl.ds(c * step, step)
        loads[c].wait()
        values = raw[part, :]
        norms = jnp.sqrt(jnp.sum(values * values, axis=1, keepdims=True) + 1e-06)
        unit[part, :] = (values * (1.0 / norms)).astype(jnp.bfloat16)
        for k in range(reps):
            store(unit.at[part], copies_ref.at[k, part])
        store(unit.at[part], payload_ref.at[part])
    loads[CHUNKS].wait()
    loads[CHUNKS + 1].wait()
    used = jnp.clip(size[0, 0] - lax.axis_index("rep") * rows, 0, rows)
    line = lax.broadcasted_iota(jnp.int32, (META, width), 0)
    meta = jnp.where(line == 0, used, 0)
    for k in range(offset_ref.shape[1]):
        meta = jnp.where(line == k + 1, offset[0, k], meta)
    unit[rows:, :] = meta.astype(jnp.float32).astype(jnp.bfloat16)
    store(unit.at[pl.ds(rows, META)], payload_ref.at[pl.ds(rows, META)])
    for copy in stores:
        copy.wait()


def row_bias(offset_ref, payload, delta, rows):
    meta = payload[rows : rows + META, 0:128].astype(jnp.float32)
    mine = jnp.float32(0.0)
    theirs = jnp.zeros((1, 128), jnp.float32)
    for k in range(offset_ref.shape[1]):
        mine = jnp.where(offset_ref[0, k] == delta, 1.0, mine)
        theirs = jnp.where(meta[k + 1 : k + 2, :] == (-delta).astype(jnp.float32), 1.0, theirs)
    paired = jnp.where(delta > 0, mine, theirs)
    line = lax.broadcasted_iota(jnp.int32, (rows, 128), 0).astype(jnp.float32)
    bias = jnp.where(line < meta[0:1, :] * paired, 0.0, -8.0)
    return jnp.concatenate([bias] * (rows // 128), axis=1)


def score(offset_ref, own_ref, payload, delta, best):
    reps, rows, _ = own_ref.shape
    bias = row_bias(offset_ref, payload, delta, rows)
    for k in range(reps):
        scores = lax.dot_general(
            payload[0:rows, :], own_ref[k], (((1,), (1,)), ((), ())), preferred_element_type=jnp.float32
        )
        best[k] = jnp.maximum(best[k], jnp.max(scores + bias, axis=0, keepdims=True))


def early_kernel(offset_ref, own_ref, ahead_ref, behind_ref, best_ref):
    reps, rows, _ = own_ref.shape
    best = [jnp.full((1, rows), -4.0, jnp.float32) for _ in range(reps)]
    score(offset_ref, own_ref, ahead_ref, jnp.int32(2), best)
    score(offset_ref, own_ref, behind_ref, jnp.int32(-2), best)
    for k in range(reps):
        best_ref[k] = best[k]


def late_kernel(
    offset_ref, own_ref, far_ref, mate_ref, ahead_ref, behind_ref, early_ref, best_ref, ahead, behind, sems
):
    reps, rows, _ = own_ref.shape
    odd = lax.rem(lax.axis_index("cluster"), 2)
    loads = [
        pltpu.make_async_copy(ahead_ref, ahead, sems.at[0]),
        pltpu.make_async_copy(behind_ref, behind, sems.at[1]),
    ]
    for load in loads:
        load.start()
    for k in range(reps):
        best_ref[k] = early_ref[k]

    def add(payload, delta):
        paired = delta < 0
        for k in range(offset_ref.shape[1]):
            paired = paired | (offset_ref[0, k] == delta)

        @pl.when(paired)
        def _():
            best = [best_ref[k] for k in range(reps)]
            score(offset_ref, own_ref, payload, delta, best)
            for k in range(reps):
                best_ref[k] = best[k]

    add(far_ref, 6 * odd - 3)
    add(mate_ref, 1 - 2 * odd)
    loads[0].wait()
    add(ahead, 3 - 2 * odd)
    loads[1].wait()
    add(behind, -1 - 2 * odd)


def over_cluster(block, even, odd):
    n = lax.axis_size("cluster")
    return lax.ppermute(block, "cluster", [((i + (odd if i % 2 else even)) % n, i) for i in range(n)])


def shards(embeddings, cluster_sizes, offsets):
    rows, width = embeddings.shape
    reps = lax.axis_size("rep")
    flat_offsets = offsets.T
    flat_sizes = cluster_sizes.reshape(1, 1)
    payload_shape = jax.ShapeDtypeStruct((rows + META, width), jnp.bfloat16)
    copies, payload = pl.pallas_call(
        norm_kernel,
        out_shape=(jax.ShapeDtypeStruct((reps, rows, width), jnp.bfloat16), payload_shape),
        in_specs=[HBM, HBM, HBM],
        out_specs=(HBM, HBM),
        scratch_shapes=[
            pltpu.SMEM(flat_sizes.shape, jnp.int32),
            pltpu.SMEM(flat_offsets.shape, jnp.int32),
            pltpu.VMEM((rows, width), jnp.float32),
            pltpu.VMEM((rows + META, width), jnp.bfloat16),
            pltpu.SemaphoreType.DMA((CHUNKS + 2,)),
            pltpu.SemaphoreType.DMA((CHUNKS * (reps + 1) + 1,)),
        ],
        name="unit_rows",
        compiler_params=WIDE,
    )(flat_sizes, flat_offsets, embeddings)
    own = lax.all_to_all(copies, "rep", 0, 0, tiled=True)
    behind = over_cluster(payload, -2, -2)
    ahead = over_cluster(payload, 2, 2)
    mate = over_cluster(payload, 1, -1)
    far = over_cluster(payload, -3, 3)
    ahead_mate = over_cluster(ahead, 1, -1)
    behind_mate = over_cluster(behind, 1, -1)
    part_shape = jax.ShapeDtypeStruct((reps, 1, rows), jnp.float32)
    part = pl.pallas_call(
        early_kernel,
        out_shape=part_shape,
        in_specs=[SMEM] + [VMEM] * 3,
        out_specs=VMEM,
        name="early_maxima",
        compiler_params=SMALL,
    )(flat_offsets, own, ahead, behind)
    part = pl.pallas_call(
        late_kernel,
        out_shape=part_shape,
        in_specs=[SMEM] + [VMEM] * 3 + [HBM] * 2 + [VMEM],
        out_specs=VMEM,
        scratch_shapes=[
            pltpu.VMEM((rows + META, width), jnp.bfloat16),
            pltpu.VMEM((rows + META, width), jnp.bfloat16),
            pltpu.SemaphoreType.DMA((2,)),
        ],
        name="late_maxima",
        compiler_params=SMALL,
    )(flat_offsets, own, far, mate, ahead_mate, behind_mate, part)
    row_best = jnp.max(lax.all_to_all(part, "rep", 0, 0, tiled=True), axis=(0, 1))
    row_ids = lax.axis_index("rep") * rows + jnp.arange(rows, dtype=jnp.int32)
    return jnp.where(row_ids < cluster_sizes[0], row_best, 0.0)


def solution(mesh):
    return jax.shard_map(
        shards,
        mesh=mesh,
        in_specs=(P(("cluster", "rep"), None), P("cluster"), P(None, "cluster")),
        out_specs=P(("cluster", "rep")),
        check_vma=False,
    )
```
